32 devices in a mesh: dp: 16 (over z, y, core), tensor: 2 (over x).
Axes of the slice: x: 2, y: 2, z: 4, core: 2. Of those that a mesh axis runs over, the one named last changes fastest.
Arguments:
- looked: bfloat16 [8192, 2048], P(('dp', 'tensor')), may hold values from -6 to 6
- column_owner: int32 [8192], replicated, may hold values from 0 to 8191, each once
- v_proj: bfloat16 [384, 8192], P(None, 'tensor'), may hold values from -0.0625 to 0.0625
- u_proj: bfloat16 [384, 8192], P(None, 'tensor'), may hold values from -0.3125 to 0.3125
- bias: float32 [8192], P('tensor'), may hold values from -3 to 3
- upstream: bfloat16 [8192, 2048], P('tensor', 'dp'), may hold values from -6 to 6
Outputs:
- d_looked: bfloat16 [8192, 2048], P(('dp', 'tensor'))
- grad_u: float32 [384, 8192], P('dp', 'tensor')
- grad_v: float32 [384, 8192], P('dp', 'tensor')
- grad_bias: float32 [8192], P('tensor')
The draws below stay inside these ranges and needn't reach their ends.
Inputs may be any that keep to these rules, and one draw needn't show every extreme that they name: A permutation of the 8192 feature columns: wire row r carries column column_owner[r].
All inputs are finite; a program needn't handle non-finite values.
Results may differ from the reference program's by a relative error of at most 0.0049.
Values may be sent and summed in bfloat16 or wider, within the bound.
A program may use at most 128 MiB of HBM per device.

```python
import math
import jax
import jax.numpy as jnp
from jax import lax

R = 384
B_DEV = 128
W = 8192
SAMPLES = 2048
N_DP = 16


def shard_levels(rng, shape, shards, low, largest):
    def one(dim, parts):
        heights = jax.random.uniform(jax.random.fold_in(jax.random.fold_in(rng, 6), dim), (parts,), jnp.float32, low / len(shards), largest / len(shards))
        return jnp.repeat(jnp.exp(heights), shape[dim] // parts).reshape((-1,) + (1,) * (len(shape) - dim - 1))

    factor_of = one(*shards[0])
    for cut in shards[1:]:
        factor_of = factor_of * one(*cut)
    return factor_of


def normal_values(key, shape, width, reach, cuts=(), kind=jnp.bfloat16):
    array = jax.random.normal(key, shape, jnp.float32) * width
    if len(cuts) > 0:
        array = shard_levels(key, shape, cuts, -0.22, 0.18) * array
    return jnp.clip(array, min=-reach, max=reach).astype(kind)


def setup_inputs(seed: int = 0) -> dict:
    seeds = jax.random.split(jax.random.key(seed), 7)
    return {
        "looked": normal_values(seeds[0], (W, SAMPLES), 1.0, 6.0, ((0, 32),)),
        "column_owner": jax.random.permutation(seeds[1], W).astype(jnp.int32),
        "v_proj": normal_values(seeds[2], (R, W), W ** -0.5, 0.0625, ((1, 2),)),
        "u_proj": normal_values(seeds[3], (R, W), R ** -0.5, 0.3125, ((1, 2),)),
        "bias": normal_values(seeds[4], (W,), 0.5, 3.0, ((0, 2),), jnp.float32),
        "upstream": normal_values(seeds[5], (W, SAMPLES), 1.0, 6.0, ((0, 2), (1, 16))),
    }


def reference(looked, column_owner, v_proj, u_proj, bias, upstream):
    norm = 1.0 / math.sqrt(SAMPLES)
    x_full = jnp.zeros_like(looked).at[column_owner].set(looked)
    group = min(N_DP, 16)
    block_size = B_DEV * group
    blocks = SAMPLES // block_size
    grad_u = jnp.zeros((R, W), jnp.float32)
    grad_v = jnp.zeros((R, W), jnp.float32)
    grad_bias = jnp.zeros((W,), jnp.float32)
    pieces = []
    for index in range(blocks):
        x_zero = x_full[:, index * block_size:(index + 1) * block_size]
        cotan = upstream[:, index * block_size:(index + 1) * block_size].astype(jnp.float32)
        hrank = jnp.dot(v_proj, x_zero, preferred_element_type=jnp.float32).astype(jnp.bfloat16)
        mix = jnp.dot(u_proj.T, hrank, preferred_element_type=jnp.float32) + bias[:, None]
        scaled = cotan * x_zero.astype(jnp.float32)
        scaled16 = scaled.astype(jnp.bfloat16)
        grad_bias = grad_bias + lax.optimization_barrier(jnp.sum(scaled, axis=1))
        grad_u = grad_u + jnp.dot(hrank, scaled16.T, preferred_element_type=jnp.float32)
        dhrank = jnp.dot(u_proj, scaled16, preferred_element_type=jnp.float32).astype(jnp.bfloat16)
        grad_v = grad_v + jnp.dot(dhrank, x_zero.T, preferred_element_type=jnp.float32)
        dx_zero = cotan * (mix + 1.0) + jnp.dot(v_proj.T, dhrank, preferred_element_type=jnp.float32)
        pieces.append(dx_zero.astype(jnp.bfloat16))
    dx_full = jnp.concatenate(pieces, axis=1)
    d_looked = jnp.take(dx_full, column_owner, axis=0)
    return (d_looked, grad_u * norm, grad_v * norm, grad_bias * norm)
```

```python
import functools
import math

import jax
import jax.numpy as jnp
from jax import lax
from jax.experimental import pallas as pl
from jax.experimental.pallas import tpu as pltpu
from jax.sharding import PartitionSpec as P

BOTH = ("dp", "tensor")


def gather_kernel(ids_ref, src_ref, out_ref, wide, picked):
    rows = out_ref.shape[0]
    wide[...] = src_ref[...].astype(jnp.float32)
    step = 32

    def body(i, carry):
        base = pl.multiple_of(i * step, step)
        for k in range(step):
            picked[pl.ds(base + k, 1), :] = wide[pl.ds(ids_ref[base + k], 1), :]
        return carry

    lax.fori_loop(0, rows // step, body, 0)
    out_ref[...] = picked[...].astype(jnp.bfloat16)


def gather_rows(ids, src, rows):
    lanes = src.shape[1]
    return pl.pallas_call(
        gather_kernel,
        out_shape=jax.ShapeDtypeStruct((rows, lanes), jnp.bfloat16),
        in_specs=[
            pl.BlockSpec(memory_space=pltpu.SMEM),
            pl.BlockSpec(memory_space=pltpu.VMEM),
        ],
        out_specs=pl.BlockSpec(memory_space=pltpu.VMEM),
        scratch_shapes=[
            pltpu.VMEM(src.shape, jnp.float32),
            pltpu.VMEM((rows, lanes), jnp.float32),
        ],
        compiler_params=pltpu.CompilerParams(vmem_limit_bytes=48 * 2**20),
        cost_estimate=pl.CostEstimate(flops=0, bytes_accessed=20 * 2**20, transcendentals=0),
    )(ids, src)


def scatter_kernel(ids_ref, src_ref, out_ref):
    rows = src_ref.shape[0]
    step = 32

    def body(i, carry):
        base = pl.multiple_of(i * step, step)
        for k in range(step):
            out_ref[pl.ds(ids_ref[base + k], 1), :] = src_ref[pl.ds(base + k, 1), :]
        return carry

    lax.fori_loop(0, rows // step, body, 0)


def scatter_rows(ids, src, rows):
    return pl.pallas_call(
        scatter_kernel,
        out_shape=jax.ShapeDtypeStruct((rows, src.shape[1]), jnp.float32),
        in_specs=[
            pl.BlockSpec(memory_space=pltpu.SMEM),
            pl.BlockSpec(memory_space=pltpu.VMEM),
        ],
        out_specs=pl.BlockSpec(memory_space=pltpu.VMEM),
        compiler_params=pltpu.CompilerParams(vmem_limit_bytes=48 * 2**20),
        cost_estimate=pl.CostEstimate(flops=0, bytes_accessed=20 * 2**20, transcendentals=0),
    )(ids, src)


def dot(left, right, dims):
    return lax.dot_general(left, right, (dims, ((), ())), preferred_element_type=jnp.float32)


def to_owner(parts, pair_count, pair_index):
    total = lax.dynamic_index_in_dim(parts, pair_index, 0, keepdims=False)
    for shift in range(1, pair_count):
        other = lax.rem(pair_index + shift, pair_count)
        sent = lax.dynamic_index_in_dim(parts, other, 0, keepdims=False)
        total = total + lax.ppermute(
            sent, "tensor", [(i, (i + shift) % pair_count) for i in range(pair_count)]
        )
    return total


def all_sum(part):
    mine = lax.psum_scatter(part, BOTH, scatter_dimension=0, tiled=True)
    return lax.all_gather(mine.astype(jnp.bfloat16), BOTH, axis=0, tiled=True)


def per_device(looked, column_owner, v_proj, u_proj, bias, upstream):
    dp_count = lax.axis_size("dp")
    pair_count = lax.axis_size("tensor")
    dp_index = lax.axis_index("dp")
    pair_index = lax.axis_index("tensor")
    own, samples = looked.shape
    rank, half = v_proj.shape
    norm = 1.0 / math.sqrt(samples)
    blocks = column_owner.reshape(dp_count, pair_count, own)

    group = lax.dynamic_index_in_dim(blocks, dp_index, 0, keepdims=False) - pair_index * half
    hit = jnp.arange(half, dtype=jnp.int32)[:, None] == group.reshape(1, -1)
    both = jnp.concatenate([v_proj, u_proj], axis=0)
    picked = jnp.dot(both, hit.astype(jnp.bfloat16), preferred_element_type=jnp.float32)
    picked = picked.astype(jnp.bfloat16).reshape(2 * rank, pair_count, own).transpose(1, 0, 2)
    params = to_owner(picked, pair_count, pair_index)
    v_own, u_own = params[:rank], params[rank:]
    bias_parts = jnp.sum(jnp.where(hit, bias[:, None], 0.0), axis=0).reshape(pair_count, own)
    bias_own = to_owner(bias_parts, pair_count, pair_index)

    paired = lax.all_gather(upstream, "tensor", axis=0, tiled=True)
    wanted = lax.dynamic_index_in_dim(blocks, pair_index, 1, keepdims=False).reshape(-1)
    wired = gather_rows(wanted, paired, half)
    cotan16 = lax.all_to_all(wired, "dp", split_axis=0, concat_axis=1, tiled=True)

    hrank = all_sum(dot(looked, v_own, ((0,), (1,))))
    cotan = cotan16.astype(jnp.float32)
    scaled = cotan * looked.astype(jnp.float32)
    scaled16 = scaled.astype(jnp.bfloat16)
    sums = jnp.sum(scaled, axis=1)
    dhrank = all_sum(dot(scaled16, u_own, ((0,), (1,))))

    mix = dot(u_own, hrank, ((0,), (1,))) + bias_own[:, None]
    d_looked = (cotan * (mix + 1.0) + dot(v_own, dhrank, ((0,), (1,)))).astype(jnp.bfloat16)

    own_u = dot(hrank, scaled16, ((0,), (1,))).reshape(dp_count, -1, own)
    own_v = dot(dhrank, looked, ((0,), (1,))).reshape(dp_count, -1, own)
    each = rank // dp_count
    fill = -(-(2 * each + 1) // 8) * 8 - 2 * each
    own_b = jnp.broadcast_to(sums[None, None, :], (dp_count, fill, own))
    sent = jnp.concatenate([own_u, own_v, own_b], axis=1) * norm
    came = lax.all_to_all(sent, "dp", split_axis=0, concat_axis=0, tiled=True)
    full = lax.all_gather(came, "tensor", axis=1, tiled=False)
    lines = full.transpose(0, 1, 3, 2).reshape(half * pair_count, -1)
    lines = jnp.pad(lines, ((0, 0), (0, 128 - lines.shape[1])))
    place = column_owner - pair_index * half
    place = jnp.where((place >= 0) & (place < half), place, half)
    spread = scatter_rows(place, lines, half + 8)[:half].T
    return (d_looked, spread[:each], spread[each : 2 * each], spread[2 * each])


def solution(mesh):
    in_specs = (
        P(BOTH, None),
        P(),
        P(None, "tensor"),
        P(None, "tensor"),
        P("tensor"),
        P("tensor", "dp"),
    )
    out_specs = (P(BOTH, None), P("dp", "tensor"), P("dp", "tensor"), P("tensor"))
    return jax.shard_map(
        per_device, mesh=mesh, in_specs=in_specs, out_specs=out_specs, check_vma=False
    )
```

```python
import functools
import math

import jax
import jax.numpy as jnp
from jax import lax
from jax.experimental import pallas as pl
from jax.experimental.pallas import tpu as pltpu
from jax.sharding import PartitionSpec as P

BOTH = ("dp", "tensor")


def gather_kernel(ids_ref, src_ref, out_ref, wide, picked):
    rows = out_ref.shape[0]
    wide[...] = src_ref[...].astype(jnp.float32)
    step = 32

    def body(i, carry):
        base = pl.multiple_of(i * step, step)
        for k in range(step):
            picked[pl.ds(base + k, 1), :] = wide[pl.ds(ids_ref[base + k], 1), :]
        return carry

    lax.fori_loop(0, rows // step, body, 0)
    out_ref[...] = picked[...].astype(jnp.bfloat16)


def gather_rows(ids, src, rows):
    lanes = src.shape[1]
    return pl.pallas_call(
        gather_kernel,
        out_shape=jax.ShapeDtypeStruct((rows, lanes), jnp.bfloat16),
        in_specs=[
            pl.BlockSpec(memory_space=pltpu.SMEM),
            pl.BlockSpec(memory_space=pltpu.VMEM),
        ],
        out_specs=pl.BlockSpec(memory_space=pltpu.VMEM),
        scratch_shapes=[
            pltpu.VMEM(src.shape, jnp.float32),
            pltpu.VMEM((rows, lanes), jnp.float32),
        ],
        compiler_params=pltpu.CompilerParams(vmem_limit_bytes=48 * 2**20),
        cost_estimate=pl.CostEstimate(flops=0, bytes_accessed=20 * 2**20, transcendentals=0),
    )(ids, src)


def scatter_kernel(ids_ref, src_ref, out_ref):
    rows = src_ref.shape[0]
    step = 32

    def body(i, carry):
        base = pl.multiple_of(i * step, step)
        for k in range(step):
            out_ref[pl.ds(ids_ref[base + k], 1), :] = src_ref[pl.ds(base + k, 1), :]
        return carry

    lax.fori_loop(0, rows // step, body, 0)


def scatter_rows(ids, src, rows):
    return pl.pallas_call(
        scatter_kernel,
        out_shape=jax.ShapeDtypeStruct((rows, src.shape[1]), jnp.float32),
        in_specs=[
            pl.BlockSpec(memory_space=pltpu.SMEM),
            pl.BlockSpec(memory_space=pltpu.VMEM),
        ],
        out_specs=pl.BlockSpec(memory_space=pltpu.VMEM),
        compiler_params=pltpu.CompilerParams(vmem_limit_bytes=48 * 2**20),
        cost_estimate=pl.CostEstimate(flops=0, bytes_accessed=20 * 2**20, transcendentals=0),
    )(ids, src)


def dot(left, right, dims):
    return lax.dot_general(left, right, (dims, ((), ())), preferred_element_type=jnp.float32)


def to_owner(parts, pair_count, pair_index):
    total = lax.dynamic_index_in_dim(parts, pair_index, 0, keepdims=False)
    for shift in range(1, pair_count):
        other = lax.rem(pair_index + shift, pair_count)
        sent = lax.dynamic_index_in_dim(parts, other, 0, keepdims=False)
        total = total + lax.ppermute(
            sent, "tensor", [(i, (i + shift) % pair_count) for i in range(pair_count)]
        )
    return total


def exchange_orders(dp_count, pair_count):
    def strides(count):
        return [1 << k for k in range(count.bit_length() - 1)]

    inner, *outer = [("dp", p) for p in strides(dp_count)]
    pair = [("tensor", p) for p in strides(pair_count)]
    return ([inner] + pair + outer, [inner] + outer[:-1] + pair + outer[-1:])


def sum_kernel(orders, part_ref, out_ref, *scratch):
    steps = len(orders[0])
    lanes = len(orders)
    took = scratch[:steps]
    given = scratch[steps : 2 * steps - 1]
    held = scratch[2 * steps - 1 : 3 * steps - 1]
    send_sem, recv_sem = scratch[3 * steps - 1 :]
    rows = part_ref.shape[0] // lanes

    def partner(axis, stride):
        me = lax.axis_index(axis)
        bit = lax.rem(me // stride, 2)
        return bit, {axis: me + stride * (1 - 2 * bit)}

    barrier = pltpu.get_barrier_semaphore()
    for axis, stride in orders[0]:
        pl.semaphore_signal(
            barrier, inc=1, device_id=partner(axis, stride)[1], device_id_type=pl.DeviceIdType.MESH
        )
    pl.semaphore_wait(barrier, steps)

    starts = [lane * rows for lane in range(lanes)]
    for k in range(steps):
        size = rows >> (k + 1)
        copies = []
        for lane in range(lanes):
            bit, device = partner(*orders[lane][k])
            away = pl.multiple_of((1 - bit) * size, size)
            if k == 0:
                source = part_ref.at[pl.ds(pl.multiple_of(lane * rows + away, size), size)]
            else:
                source = given[k - 1].at[lane]
                source[...] = held[k - 1][lane, pl.ds(away, size), :].astype(jnp.bfloat16)
            copy = pltpu.make_async_remote_copy(
                src_ref=source,
                dst_ref=took[k].at[lane],
                send_sem=send_sem.at[lane, k],
                recv_sem=recv_sem.at[lane, k],
                device_id=device,
                device_id_type=pl.DeviceIdType.MESH,
            )
            copy.start()
            copies.append(copy)
        for lane in range(lanes):
            bit, _ = partner(*orders[lane][k])
            kept = pl.multiple_of(bit * size, size)
            copies[lane].wait()
            if k == 0:
                own = part_ref[pl.ds(pl.multiple_of(lane * rows + kept, size), size), :]
            else:
                own = held[k - 1][lane, pl.ds(kept, size), :]
            held[k][lane] = own + took[k][lane].astype(jnp.float32)
            starts[lane] = starts[lane] + kept

    size = rows >> steps
    for lane in range(lanes):
        out_ref[pl.ds(pl.multiple_of(starts[lane], size), size), :] = held[-1][lane].astype(
            jnp.bfloat16
        )
    for k in reversed(range(steps)):
        size = rows >> (k + 1)
        copies = []
        for lane in range(lanes):
            bit, device = partner(*orders[lane][k])
            piece = out_ref.at[pl.ds(pl.multiple_of(starts[lane], size), size)]
            copy = pltpu.make_async_remote_copy(
                src_ref=piece,
                dst_ref=piece,
                send_sem=send_sem.at[lane, steps + k],
                recv_sem=recv_sem.at[lane, steps + k],
                device_id=device,
                device_id_type=pl.DeviceIdType.MESH,
            )
            copy.start()
            copies.append(copy)
            starts[lane] = starts[lane] - bit * size
        for copy in copies:
            copy.wait()


def all_sum(part, dp_count, pair_count):
    orders = exchange_orders(dp_count, pair_count)
    steps, lanes = len(orders[0]), len(orders)
    samples, rank = part.shape
    chunk = min(samples, max(2048, (16 * lanes) << steps))
    rows = chunk // lanes

    def shapes(kind, first, last):
        return [pltpu.VMEM((lanes, rows >> (k + 1), rank), kind) for k in range(first, last)]

    call = pl.pallas_call(
        functools.partial(sum_kernel, orders),
        out_shape=jax.ShapeDtypeStruct((chunk, rank), jnp.bfloat16),
        in_specs=[pl.BlockSpec(memory_space=pltpu.VMEM)],
        out_specs=pl.BlockSpec(memory_space=pltpu.VMEM),
        scratch_shapes=[
            *shapes(jnp.float32, 0, 1),
            *shapes(jnp.bfloat16, 1, steps),
            *shapes(jnp.bfloat16, 1, steps),
            *shapes(jnp.float32, 0, steps),
            pltpu.SemaphoreType.DMA((lanes, 2 * steps)),
            pltpu.SemaphoreType.DMA((lanes, 2 * steps)),
        ],
        compiler_params=pltpu.CompilerParams(
            collective_id=1, has_side_effects=True, vmem_limit_bytes=56 * 2**20
        ),
        cost_estimate=pl.CostEstimate(
            flops=samples * rank, bytes_accessed=30 * 2**20, transcendentals=0
        ),
    )
    pieces = [call(part[at : at + chunk]) for at in range(0, samples, chunk)]
    return jnp.concatenate(pieces, axis=0) if len(pieces) > 1 else pieces[0]


def per_device(looked, column_owner, v_proj, u_proj, bias, upstream):
    dp_count = lax.axis_size("dp")
    pair_count = lax.axis_size("tensor")
    dp_index = lax.axis_index("dp")
    pair_index = lax.axis_index("tensor")
    own, samples = looked.shape
    rank, half = v_proj.shape
    norm = 1.0 / math.sqrt(samples)
    blocks = column_owner.reshape(dp_count, pair_count, own)

    group = lax.dynamic_index_in_dim(blocks, dp_index, 0, keepdims=False) - pair_index * half
    hit = jnp.arange(half, dtype=jnp.int32)[:, None] == group.reshape(1, -1)
    both = jnp.concatenate([v_proj, u_proj], axis=0)
    picked = jnp.dot(both, hit.astype(jnp.bfloat16), preferred_element_type=jnp.float32)
    picked = picked.astype(jnp.bfloat16).reshape(2 * rank, pair_count, own).transpose(1, 0, 2)
    params = to_owner(picked, pair_count, pair_index)
    v_own, u_own = params[:rank], params[rank:]
    bias_parts = jnp.sum(jnp.where(hit, bias[:, None], 0.0), axis=0).reshape(pair_count, own)
    bias_own = to_owner(bias_parts, pair_count, pair_index)

    paired = lax.all_gather(upstream, "tensor", axis=0, tiled=True)
    wanted = lax.dynamic_index_in_dim(blocks, pair_index, 1, keepdims=False).reshape(-1)
    wired = gather_rows(wanted, paired, half)
    cotan16 = lax.all_to_all(wired, "dp", split_axis=0, concat_axis=1, tiled=True)

    hrank = all_sum(dot(looked, v_own, ((0,), (1,))), dp_count, pair_count)
    cotan = cotan16.astype(jnp.float32)
    scaled = cotan * looked.astype(jnp.float32)
    scaled16 = scaled.astype(jnp.bfloat16)
    sums = jnp.sum(scaled, axis=1)
    dhrank = all_sum(dot(scaled16, u_own, ((0,), (1,))), dp_count, pair_count)

    mix = dot(u_own, hrank, ((0,), (1,))) + bias_own[:, None]
    d_looked = (cotan * (mix + 1.0) + dot(v_own, dhrank, ((0,), (1,)))).astype(jnp.bfloat16)

    own_u = dot(hrank, scaled16, ((0,), (1,))).reshape(dp_count, -1, own)
    own_v = dot(dhrank, looked, ((0,), (1,))).reshape(dp_count, -1, own)
    each = rank // dp_count
    fill = -(-(2 * each + 1) // 8) * 8 - 2 * each
    own_b = jnp.broadcast_to(sums[None, None, :], (dp_count, fill, own))
    sent = jnp.concatenate([own_u, own_v, own_b], axis=1) * norm
    came = lax.all_to_all(sent, "dp", split_axis=0, concat_axis=0, tiled=True)
    full = lax.all_gather(came, "tensor", axis=1, tiled=False)
    lines = full.transpose(0, 1, 3, 2).reshape(half * pair_count, -1)
    lines = jnp.pad(lines, ((0, 0), (0, 128 - lines.shape[1])))
    place = column_owner - pair_index * half
    place = jnp.where((place >= 0) & (place < half), place, half)
    spread = scatter_rows(place, lines, half + 8)[:half].T
    return (d_looked, spread[:each], spread[each : 2 * each], spread[2 * each])


def solution(mesh):
    in_specs = (
        P(BOTH, None),
        P(),
        P(None, "tensor"),
        P(None, "tensor"),
        P("tensor"),
        P("tensor", "dp"),
    )
    out_specs = (P(BOTH, None), P("dp", "tensor"), P("dp", "tensor"), P("tensor"))
    return jax.shard_map(
        per_device, mesh=mesh, in_specs=in_specs, out_specs=out_specs, check_vma=False
    )
```

```python
import functools
import math

import jax
import jax.numpy as jnp
from jax import lax
from jax.experimental import pallas as pl
from jax.experimental.pallas import tpu as pltpu
from jax.sharding import PartitionSpec as P

BOTH = ("dp", "tensor")


def gather_kernel(ids_ref, src_ref, out_ref, wide, picked):
    rows = out_ref.shape[0]
    wide[...] = src_ref[...].astype(jnp.float32)
    step = 32

    def body(i, carry):
        base = pl.multiple_of(i * step, step)
        for k in range(step):
            picked[pl.ds(base + k, 1), :] = wide[pl.ds(ids_ref[base + k], 1), :]
        return carry

    lax.fori_loop(0, rows // step, body, 0)
    out_ref[...] = picked[...].astype(jnp.bfloat16)


def gather_rows(ids, src, rows):
    lanes = src.shape[1]
    return pl.pallas_call(
        gather_kernel,
        out_shape=jax.ShapeDtypeStruct((rows, lanes), jnp.bfloat16),
        in_specs=[
            pl.BlockSpec(memory_space=pltpu.SMEM),
            pl.BlockSpec(memory_space=pltpu.VMEM),
        ],
        out_specs=pl.BlockSpec(memory_space=pltpu.VMEM),
        scratch_shapes=[
            pltpu.VMEM(src.shape, jnp.float32),
            pltpu.VMEM((rows, lanes), jnp.float32),
        ],
        compiler_params=pltpu.CompilerParams(vmem_limit_bytes=48 * 2**20),
        cost_estimate=pl.CostEstimate(flops=0, bytes_accessed=20 * 2**20, transcendentals=0),
    )(ids, src)


def scatter_kernel(ids_ref, src_ref, out_ref):
    rows = src_ref.shape[0]
    step = 32

    def body(i, carry):
        base = pl.multiple_of(i * step, step)
        for k in range(step):
            out_ref[pl.ds(ids_ref[base + k], 1), :] = src_ref[pl.ds(base + k, 1), :]
        return carry

    lax.fori_loop(0, rows // step, body, 0)


def scatter_rows(ids, src, rows):
    return pl.pallas_call(
        scatter_kernel,
        out_shape=jax.ShapeDtypeStruct((rows, src.shape[1]), jnp.float32),
        in_specs=[
            pl.BlockSpec(memory_space=pltpu.SMEM),
            pl.BlockSpec(memory_space=pltpu.VMEM),
        ],
        out_specs=pl.BlockSpec(memory_space=pltpu.VMEM),
        compiler_params=pltpu.CompilerParams(vmem_limit_bytes=48 * 2**20),
        cost_estimate=pl.CostEstimate(flops=0, bytes_accessed=20 * 2**20, transcendentals=0),
    )(ids, src)


def dot(left, right, dims):
    return lax.dot_general(left, right, (dims, ((), ())), preferred_element_type=jnp.float32)


def to_owner(parts, pair_count, pair_index):
    total = lax.dynamic_index_in_dim(parts, pair_index, 0, keepdims=False)
    for shift in range(1, pair_count):
        other = lax.rem(pair_index + shift, pair_count)
        sent = lax.dynamic_index_in_dim(parts, other, 0, keepdims=False)
        total = total + lax.ppermute(
            sent, "tensor", [(i, (i + shift) % pair_count) for i in range(pair_count)]
        )
    return total


def exchange_orders(dp_count, pair_count):
    def strides(count):
        return [1 << k for k in range(count.bit_length() - 1)]

    inner, *outer = [("dp", p) for p in strides(dp_count)]
    pair = [("tensor", p) for p in strides(pair_count)]
    return ([inner] + pair + outer, [inner] + outer[:-1] + pair + outer[-1:])


def sum_kernel(orders, part_ref, out_ref, *scratch):
    steps = len(orders[0])
    lanes = len(orders)
    took = scratch[:steps]
    given = scratch[steps : 2 * steps - 1]
    held = scratch[2 * steps - 1 : 3 * steps - 1]
    send_sem, recv_sem = scratch[3 * steps - 1 :]
    rows = part_ref.shape[0] // lanes

    def partner(axis, stride):
        me = lax.axis_index(axis)
        bit = lax.rem(me // stride, 2)
        return bit, {axis: me + stride * (1 - 2 * bit)}

    barrier = pltpu.get_barrier_semaphore()
    for axis, stride in orders[0]:
        pl.semaphore_signal(
            barrier, inc=1, device_id=partner(axis, stride)[1], device_id_type=pl.DeviceIdType.MESH
        )
    pl.semaphore_wait(barrier, steps)

    starts = [lane * rows for lane in range(lanes)]
    for k in range(steps):
        size = rows >> (k + 1)
        copies = []
        for lane in range(lanes):
            bit, device = partner(*orders[lane][k])
            away = pl.multiple_of((1 - bit) * size, size)
            if k == 0:
                source = part_ref.at[pl.ds(pl.multiple_of(lane * rows + away, size), size)]
            else:
                source = given[k - 1].at[lane]
                source[...] = held[k - 1][lane, pl.ds(away, size), :].astype(jnp.bfloat16)
            copy = pltpu.make_async_remote_copy(
                src_ref=source,
                dst_ref=took[k].at[lane],
                send_sem=send_sem.at[lane, k],
                recv_sem=recv_sem.at[lane, k],
                device_id=device,
                device_id_type=pl.DeviceIdType.MESH,
            )
            copy.start()
            copies.append(copy)
        for lane in range(lanes):
            bit, _ = partner(*orders[lane][k])
            kept = pl.multiple_of(bit * size, size)
            copies[lane].wait()
            if k == 0:
                own = part_ref[pl.ds(pl.multiple_of(lane * rows + kept, size), size), :]
            else:
                own = held[k - 1][lane, pl.ds(kept, size), :]
            held[k][lane] = own + took[k][lane].astype(jnp.float32)
            starts[lane] = starts[lane] + kept

    size = rows >> steps
    for lane in range(lanes):
        out_ref[pl.ds(pl.multiple_of(starts[lane], size), size), :] = held[-1][lane].astype(
            jnp.bfloat16
        )
    for k in reversed(range(steps)):
        size = rows >> (k + 1)
        copies = []
        for lane in range(lanes):
            bit, device = partner(*orders[lane][k])
            piece = out_ref.at[pl.ds(pl.multiple_of(starts[lane], size), size)]
            copy = pltpu.make_async_remote_copy(
                src_ref=piece,
                dst_ref=piece,
                send_sem=send_sem.at[lane, steps + k],
                recv_sem=recv_sem.at[lane, steps + k],
                device_id=device,
                device_id_type=pl.DeviceIdType.MESH,
            )
            copy.start()
            copies.append(copy)
            starts[lane] = starts[lane] - bit * size
        for copy in copies:
            copy.wait()


def all_sum(part, dp_count, pair_count):
    orders = exchange_orders(dp_count, pair_count)
    steps, lanes = len(orders[0]), len(orders)
    samples, rank = part.shape
    chunk = min(samples, max(2048, (16 * lanes) << steps))
    rows = chunk // lanes

    def shapes(kind, first, last):
        return [pltpu.VMEM((lanes, rows >> (k + 1), rank), kind) for k in range(first, last)]

    call = pl.pallas_call(
        functools.partial(sum_kernel, orders),
        out_shape=jax.ShapeDtypeStruct((chunk, rank), jnp.bfloat16),
        in_specs=[pl.BlockSpec(memory_space=pltpu.VMEM)],
        out_specs=pl.BlockSpec(memory_space=pltpu.VMEM),
        scratch_shapes=[
            *shapes(jnp.float32, 0, 1),
            *shapes(jnp.bfloat16, 1, steps),
            *shapes(jnp.bfloat16, 1, steps),
            *shapes(jnp.float32, 0, steps),
            pltpu.SemaphoreType.DMA((lanes, 2 * steps)),
            pltpu.SemaphoreType.DMA((lanes, 2 * steps)),
        ],
        compiler_params=pltpu.CompilerParams(
            collective_id=1, has_side_effects=True, vmem_limit_bytes=56 * 2**20
        ),
        cost_estimate=pl.CostEstimate(
            flops=samples * rank, bytes_accessed=150 * 2**20, transcendentals=0
        ),
    )
    pieces = [call(part[at : at + chunk]) for at in range(0, samples, chunk)]
    return jnp.concatenate(pieces, axis=0) if len(pieces) > 1 else pieces[0]


def per_device(looked, column_owner, v_proj, u_proj, bias, upstream):
    dp_count = lax.axis_size("dp")
    pair_count = lax.axis_size("tensor")
    dp_index = lax.axis_index("dp")
    pair_index = lax.axis_index("tensor")
    own, samples = looked.shape
    rank, half = v_proj.shape
    norm = 1.0 / math.sqrt(samples)
    blocks = column_owner.reshape(dp_count, pair_count, own)

    group = lax.dynamic_index_in_dim(blocks, dp_index, 0, keepdims=False) - pair_index * half
    hit = jnp.arange(half, dtype=jnp.int32)[:, None] == group.reshape(1, -1)
    both = jnp.concatenate([v_proj, u_proj], axis=0)
    picked = jnp.dot(both, hit.astype(jnp.bfloat16), preferred_element_type=jnp.float32)
    picked = picked.astype(jnp.bfloat16).reshape(2 * rank, pair_count, own).transpose(1, 0, 2)
    params = to_owner(picked, pair_count, pair_index)
    v_own, u_own = params[:rank], params[rank:]
    bias_parts = jnp.sum(jnp.where(hit, bias[:, None], 0.0), axis=0).reshape(pair_count, own)
    bias_own = to_owner(bias_parts, pair_count, pair_index)

    paired = lax.all_gather(upstream, "tensor", axis=0, tiled=True)
    paired, v_own, u_own = lax.optimization_barrier((paired, v_own, u_own))
    wanted = lax.dynamic_index_in_dim(blocks, pair_index, 1, keepdims=False).reshape(-1)
    wired = gather_rows(wanted, paired, half)
    cotan16 = lax.all_to_all(wired, "dp", split_axis=0, concat_axis=1, tiled=True)

    hrank = all_sum(dot(looked, v_own, ((0,), (1,))), dp_count, pair_count)
    cotan = cotan16.astype(jnp.float32)
    scaled = cotan * looked.astype(jnp.float32)
    scaled16 = scaled.astype(jnp.bfloat16)
    sums = jnp.sum(scaled, axis=1)
    dh_part = dot(scaled16, u_own, ((0,), (1,)))

    each = rank // dp_count
    fill = -(-(each + 3) // 8) * 8 - each
    terms, rest = [], sums * norm
    for _ in range(3):
        term = lax.reduce_precision(rest, exponent_bits=8, mantissa_bits=7)
        terms.append(term.astype(jnp.bfloat16))
        rest = rest - term
    own_b = jnp.pad(jnp.stack(terms), ((0, fill - 3), (0, 0)))
    own_b = jnp.broadcast_to(own_b[None], (dp_count, fill, own))
    own_u = (dot(hrank, scaled16, ((0,), (1,))) * norm).astype(jnp.bfloat16)
    own_u = jnp.concatenate([own_u.reshape(dp_count, each, own), own_b], axis=1)
    dh_part, own_u = lax.optimization_barrier((dh_part, own_u))
    came_u = lax.all_to_all(own_u, "dp", split_axis=0, concat_axis=0, tiled=True)
    dhrank = all_sum(dh_part, dp_count, pair_count)
    own_v = (dot(dhrank, looked, ((0,), (1,))) * norm).astype(jnp.bfloat16)
    own_v = own_v.reshape(dp_count, each, own)
    mix = dot(u_own, hrank, ((0,), (1,))) + bias_own[:, None]
    d_looked = (cotan * (mix + 1.0) + dot(v_own, dhrank, ((0,), (1,)))).astype(jnp.bfloat16)
    fulls = []
    came_v = lax.all_to_all(own_v, "dp", split_axis=0, concat_axis=0, tiled=True)
    for came in (came_u, came_v):
        fulls.append(lax.all_gather(came, "tensor", axis=1, tiled=False))
    full = jnp.concatenate(fulls, axis=2).astype(jnp.float32)
    lines = full.transpose(0, 1, 3, 2).reshape(half * pair_count, -1)
    lines = jnp.pad(lines, ((0, 0), (0, 128 - lines.shape[1])))
    place = column_owner - pair_index * half
    place = jnp.where((place >= 0) & (place < half), place, half)
    spread = scatter_rows(place, lines, half + 8)[:half].T
    grad_bias = jnp.sum(spread[each : each + 3], axis=0)
    grad_v = spread[each + fill : 2 * each + fill]
    return (d_looked, spread[:each], grad_v, grad_bias)


def solution(mesh):
    in_specs = (
        P(BOTH, None),
        P(),
        P(None, "tensor"),
        P(None, "tensor"),
        P("tensor"),
        P("tensor", "dp"),
    )
    out_specs = (P(BOTH, None), P("dp", "tensor"), P("dp", "tensor"), P("tensor"))
    return jax.shard_map(
        per_device, mesh=mesh, in_specs=in_specs, out_specs=out_specs, check_vma=False
    )
```
